32 devices in a mesh: tok: 4 (over z), seq: 8 (over y, x, core).
Axes of the slice: x: 2, y: 2, z: 4, core: 2. Of those that a mesh axis runs over, the one named last changes fastest.
Arguments:
- keys: bfloat16 [8, 2, 4096, 512], P('seq', None, 'tok'), may hold values from -6 to 6
- values: bfloat16 [8, 2, 4096, 512], P('seq', None, 'tok'), may hold values from -6 to 6
- queries: bfloat16 [8, 2, 4096, 512], P('seq', None, 'tok'), may hold values from -6 to 6
- token_rate: float32 [8, 2, 4096], P('seq', None, 'tok'), may hold values from 0.1 to 1
- valid_count: int32 [8, 2], P('seq'), may hold values from 2048 to 4096
- loss_scale: float32 [1], replicated, may hold values from 128 to 2048
- w_gate: bfloat16 [512, 512], replicated, may hold values from -0.25 to 0.25
- w_up: bfloat16 [512, 512], replicated, may hold values from -0.25 to 0.25
- w_down: bfloat16 [512, 512], replicated, may hold values from -0.25 to 0.25
- out_cotangent: bfloat16 [8, 2, 4096, 512], P('seq', None, 'tok'), may hold values from -0.125 to 0.125
Outputs:
- fast_out: bfloat16 [8, 2, 4096, 512], P('seq', None, 'tok')
- grad_gate: float32 [512, 512], P(None, 'tok')
- grad_up: float32 [512, 512], P(None, 'tok')
- grad_down: float32 [512, 512], P('tok')
- levels: float32 [2, 512], P(None, 'tok')
The draws below stay inside these ranges and needn't reach their ends.
All inputs are finite; a program needn't handle non-finite values.
Results may differ from the reference program's by a relative error of at most 0.0087.
Values may be sent and summed in bfloat16 or wider, within the bound.
A program may use at most 128 MiB of HBM per device.

```python
import math
import jax
import jax.numpy as jnp
from jax import lax

D = 512
HID = 512
BLOCKS = 2
BLOCK_LEN = 4096
SEQS = 8
ALL_TOKENS = 65536


def with_ends(array, own_key, least, largest):
    longest = array.shape.index(max(array.shape))
    spots = []
    for shift in (0, 1):
        where = [jax.random.randint(jax.random.fold_in(own_key, axis), (), 0, length) for axis, length in enumerate(array.shape)]
        where[longest] = (where[longest] + shift) % array.shape[longest]
        spots.append(tuple(where))
    return array.at[spots[0]].set(least).at[spots[1]].set(largest)


def steps_of(rng, extent, pieces, low, high):
    factor_of = 1.0
    for dim, shards_of in pieces:
        heights = jax.random.uniform(jax.random.fold_in(jax.random.fold_in(rng, 6), dim), (shards_of,), jnp.float32, low / len(pieces), high / len(pieces))
        factor_of = factor_of * jnp.repeat(jnp.exp(heights), extent[dim] // shards_of).reshape((-1,) + (1,) * (len(extent) - 1 - dim))
    return factor_of


def scatter_about(rng, extent, spread, bound, cuts=(), kind=jnp.bfloat16):
    entries = jax.random.normal(rng, extent, jnp.float32) * spread
    if len(cuts) > 0:
        entries = steps_of(rng, extent, cuts, -0.22, 0.18) * entries
    return jnp.clip(entries, min=-bound, max=bound).astype(kind)


def setup_inputs(seed: int = 0) -> dict:
    key_list = jax.random.split(jax.random.key(seed), 11)
    keys = scatter_about(key_list[0], (SEQS, BLOCKS, BLOCK_LEN, D), 1.0, 6.0, ((0, 8), (2, 4)))
    values = scatter_about(key_list[1], (SEQS, BLOCKS, BLOCK_LEN, D), 1.0, 6.0, ((0, 8), (2, 4)))
    queries = scatter_about(key_list[2], (SEQS, BLOCKS, BLOCK_LEN, D), 1.0, 6.0, ((0, 8), (2, 4)))
    token_rate = jnp.clip(jnp.exp(math.log(1.0) - 2.3025851 * jax.random.uniform(key_list[3], (SEQS, BLOCKS, BLOCK_LEN), jnp.float32) ** steps_of(key_list[3], (SEQS, BLOCKS, BLOCK_LEN), ((0, 8), (2, 4)), -0.2, 0.2)), 0.1, 1.0)
    valid_count = with_ends(jax.random.randint(key_list[4], (SEQS, BLOCKS), BLOCK_LEN // 2, BLOCK_LEN + 1), jax.random.fold_in(key_list[4], 1), BLOCK_LEN // 2, BLOCK_LEN).astype(jnp.int32)
    loss_scale = jnp.clip(jnp.exp(jax.random.uniform(key_list[5], (1,), jnp.float32, math.log(128.0), math.log(2048.0))), 128.0, 2048.0)
    w_gate = scatter_about(key_list[6], (D, HID), D ** -0.5, 0.25)
    w_up = scatter_about(key_list[7], (D, HID), D ** -0.5, 0.25)
    w_down = scatter_about(key_list[8], (HID, D), HID ** -0.5, 0.25)
    out_cotangent = scatter_about(key_list[9], (SEQS, BLOCKS, BLOCK_LEN, D), (2.0 * ALL_TOKENS ** -0.5), 0.125, ((0, 8), (2, 4)))
    return {"keys": keys, "values": values, "queries": queries, "token_rate": token_rate, "valid_count": valid_count, "loss_scale": loss_scale, "w_gate": w_gate, "w_up": w_up, "w_down": w_down, "out_cotangent": out_cotangent}


momentum_keep = 0.9
step_rate = 3.0
tiny_value = 1e-06

def forward(inputs, gate_w, up_w):
    gate = jnp.dot(inputs, gate_w, preferred_element_type=jnp.float32)
    upper = jnp.dot(inputs, up_w, preferred_element_type=jnp.float32)
    hidden = (jax.nn.silu(gate) * upper).astype(jnp.bfloat16)
    return (gate, upper, hidden)

def backward(inputs, gate, upper, hidden, down_w, cotan):
    grad_down = jnp.dot(hidden.T, cotan, preferred_element_type=jnp.float32)
    back = jnp.dot(cotan, down_w.T, preferred_element_type=jnp.float32)
    sigma = jax.nn.sigmoid(gate)
    d_upper = (back * gate * sigma).astype(jnp.bfloat16)
    d_gate = (back * upper * sigma * (1.0 + gate * (1.0 - sigma))).astype(jnp.bfloat16)
    grad_gate = jnp.dot(inputs.T, d_gate, preferred_element_type=jnp.float32)
    grad_up = jnp.dot(inputs.T, d_upper, preferred_element_type=jnp.float32)
    return (grad_gate, grad_up, grad_down)

def renorm(gate_w, up_w, down_w, gate_n, up_n, down_n):
    gate_w = gate_w * (gate_n / jnp.sqrt(lax.optimization_barrier(jnp.sum(gate_w * gate_w, axis=0)) + tiny_value))
    up_w = up_w * (up_n / jnp.sqrt(lax.optimization_barrier(jnp.sum(up_w * up_w, axis=0)) + tiny_value))
    down_w = down_w * (down_n / jnp.sqrt(lax.optimization_barrier(jnp.sum(down_w * down_w, axis=1)) + tiny_value))[:, None]
    return (gate_w, up_w, down_w)

def reference(keys, values, queries, token_rate, valid_count, loss_scale, w_gate, w_up, w_down, out_cotangent):
    scale = loss_scale[0]
    gate_full = w_gate.astype(jnp.float32)
    up_full = w_up.astype(jnp.float32)
    down_full = w_down.astype(jnp.float32)
    gate_n = jnp.sqrt(lax.optimization_barrier(jnp.sum(gate_full * gate_full, axis=0)) + tiny_value)
    up_n = jnp.sqrt(lax.optimization_barrier(jnp.sum(up_full * up_full, axis=0)) + tiny_value)
    down_n = jnp.sqrt(lax.optimization_barrier(jnp.sum(down_full * down_full, axis=1)) + tiny_value)
    positions = jnp.arange(BLOCK_LEN, dtype=jnp.int32)

    def one_sequence(items):
        key_seq, value_seq, query_seq, rate_seq, count_seq, cot_seq = items
        state = (gate_full, up_full, down_full)
        momentum = tuple((jnp.zeros_like(entry) for entry in state))
        totals = tuple((jnp.zeros_like(entry) for entry in state))
        current = (w_gate, w_up, w_down)
        level_list = []
        output_list = []
        for index in range(BLOCKS):
            count = count_seq[index]
            mask = (positions < count).astype(jnp.float32)
            inputs = key_seq[index]
            gate, upper, hidden = forward(inputs, current[0], current[1])
            factor = -(scale * rate_seq[index] * mask / count.astype(jnp.float32))
            cotan = (factor[:, None] * value_seq[index].astype(jnp.float32)).astype(jnp.bfloat16)
            summed = backward(inputs, gate, upper, hidden, current[2], cotan)
            level_list.append(lax.optimization_barrier(jnp.max(jnp.abs(summed[0]), axis=0)))
            momentum = tuple((momentum_keep * held + grad / scale for held, grad in zip(momentum, summed)))
            stepped = tuple((entry - step_rate * held for entry, held in zip(state, momentum)))
            state = renorm(stepped[0], stepped[1], stepped[2], gate_n, up_n, down_n)
            current = tuple((entry.astype(jnp.bfloat16) for entry in state))
            inputs = query_seq[index]
            gate, upper, hidden = forward(inputs, current[0], current[1])
            result = jnp.dot(hidden, current[2], preferred_element_type=jnp.float32)
            output_list.append((result * mask[:, None]).astype(jnp.bfloat16))
            outer_cot = cot_seq[index] * mask[:, None].astype(jnp.bfloat16)
            partial_grads = backward(inputs, gate, upper, hidden, current[2], outer_cot)
            totals = tuple((held + grad for held, grad in zip(totals, partial_grads)))
        return (jnp.stack(output_list), totals[0], totals[1], totals[2], jnp.stack(level_list))
    results = lax.map(one_sequence, (keys, values, queries, token_rate, valid_count, out_cotangent))
    fast_out = results[0]
    grad_gate = lax.optimization_barrier(jnp.sum(results[1], axis=0))
    grad_up = lax.optimization_barrier(jnp.sum(results[2], axis=0))
    grad_down = lax.optimization_barrier(jnp.sum(results[3], axis=0))
    levels = lax.optimization_barrier(jnp.max(results[4], axis=0))
    return (fast_out, grad_gate, grad_up, grad_down, levels)
```

```python
import functools

import jax
import jax.numpy as jnp
from jax import lax
from jax.experimental import pallas as pl
from jax.experimental.pallas import tpu as pltpu
from jax.sharding import PartitionSpec as P

momentum_keep = 0.9
step_rate = 3.0
tiny_value = 1e-06
MESH = pl.DeviceIdType.MESH
f32 = jnp.float32
bf16 = jnp.bfloat16


def dot_nt(a, b):
    return lax.dot_general(a, b, (((1,), (1,)), ((), ())), preferred_element_type=f32)


def dot_nn(a, b):
    return lax.dot_general(a, b, (((1,), (0,)), ((), ())), preferred_element_type=f32)


def dot_tn(a, b):
    return lax.dot_general(a, b, (((0,), (0,)), ((), ())), preferred_element_type=f32)


def plan_stages(nseq, piece, width):
    stages = []
    q, w, bit = piece, width, 1
    while bit < nseq:
        if w > 128:
            w //= 2
            stages.append((bit, "lane", q, w))
        else:
            q //= 2
            stages.append((bit, "unit", q, w))
        bit *= 2
    return stages, q, w


def kernel(
    n, nseq, chunks, unit, stages,
    scale_ref, keys, values, queries, cots, w_init, rows_ref,
    out_hbm, grad_ref, level_ref,
    kv, vv, qv, cv, w, sbuf, rbuf, state, mom, acc, tot, hid, fo, lev, levr, zs, zr, gat, *rest,
):
    ns = len(stages)
    sb, rb = rest[:ns], rest[ns:2 * ns]
    in_sem, s_send, s_recv, w_send, w_recv, o_sem, f_send, f_recv, l_send, l_recv, g_send, g_recv, z_send, z_recv, y_send, y_recv = rest[2 * ns:]
    dim = kv.shape[2]
    tokens = kv.shape[1]
    piece = chunks * unit // n
    me = lax.axis_index("tok")
    seq = lax.axis_index("seq")
    half = n // 2
    low = me < half
    inn = jnp.where(low, me + 1, me - 1)
    mid = jnp.logical_or(me == half - 1, me == half)
    has_out = jnp.logical_and(me > 0, me < n - 1)
    out = jnp.where(low, jnp.maximum(me - 1, 0), jnp.minimum(me + 1, n - 1))
    kind = jnp.where(mid, 1, 0)

    first_in = [
        pltpu.make_async_copy(keys.at[0], kv.at[0], in_sem.at[0]),
        pltpu.make_async_copy(w_init, w.at[pl.ds(0, chunks)], in_sem.at[1]),
        pltpu.make_async_copy(values.at[0], vv.at[0], in_sem.at[2]),
    ]
    later_in = [
        pltpu.make_async_copy(keys.at[1], kv.at[1], in_sem.at[3]),
        pltpu.make_async_copy(values.at[1], vv.at[1], in_sem.at[4]),
        pltpu.make_async_copy(queries, qv, in_sem.at[5]),
        pltpu.make_async_copy(cots, cv, in_sem.at[6]),
    ]
    for copy in first_in + later_in:
        copy.start()

    barrier = pltpu.get_barrier_semaphore()
    for d in range(1, n):
        pl.semaphore_signal(barrier, inc=1, device_id={"tok": lax.rem(me + d, n)}, device_id_type=MESH)
    partners = []
    for bit, _, _, _ in stages:
        side = lax.rem(seq // bit, 2)
        partner = seq + bit * (1 - 2 * side)
        partners.append((side, partner))
        pl.semaphore_signal(barrier, inc=1, device_id={"seq": partner}, device_id_type=MESH)
    pl.semaphore_wait(barrier, n - 1 + ns)

    lev[...] = jnp.zeros_like(lev)
    for copy in first_in:
        copy.wait()
    scale = scale_ref[0]

    @pl.when(mid)
    def _():
        def fill(c, carry):
            state[c] = w[c].astype(f32)
            mom[c] = jnp.zeros(mom.shape[1:], f32)
            return carry
        lax.fori_loop(0, chunks, fill, 0)

    def send_copy(t):
        return pltpu.make_async_remote_copy(
            src_ref=sbuf.at[t], dst_ref=rbuf.at[kind, t], send_sem=s_send.at[t],
            recv_sem=s_recv.at[kind, t], device_id={"tok": inn}, device_id_type=MESH)

    def recv_copy(k, t):
        return pltpu.make_async_remote_copy(
            src_ref=sbuf.at[t], dst_ref=rbuf.at[k, t], send_sem=s_send.at[t],
            recv_sem=s_recv.at[k, t], device_id={"tok": inn}, device_id_type=MESH)

    def weight_copy(t):
        return pltpu.make_async_remote_copy(
            src_ref=w.at[t + chunks], dst_ref=w.at[t + chunks], send_sem=w_send.at[t],
            recv_sem=w_recv.at[t], device_id={"tok": out}, device_id_type=MESH)

    def parts(wt, x, e, row):
        ab = dot_nt(w[wt, 0:2].reshape(2 * unit, dim), x)
        r = dot_nt(w[wt, 2], e) * row
        a, b = ab[:unit], ab[unit:]
        s = jax.nn.sigmoid(a)
        g = a * s
        h = (g * b * row).astype(bf16)
        eb = (r * g).astype(bf16)
        ea = (r * b * s * (1.0 + a * (1.0 - s))).astype(bf16)
        gg = dot_nn(jnp.concatenate([ea, eb], axis=0), x)
        gw = dot_nn(h, e)
        return h, gg, gw

    def finish(t):
        c = lax.rem(t, chunks)
        recv_copy(1, t).wait_recv()
        s = sbuf[t].astype(f32) + rbuf[1, t].astype(f32)
        top = jnp.abs(s[0])
        top = functools.reduce(jnp.maximum, [top[:, k:k + 128] for k in range(0, dim, 128)])
        lev[t] = jnp.max(top.T, axis=0, keepdims=True)
        m = momentum_keep * mom[c] + s * (1.0 / scale)
        mom[c] = m
        first = w[c].astype(f32)
        ref_norm = jnp.sqrt(jnp.sum(first * first, axis=2, keepdims=True) + tiny_value)
        st = state[c] - step_rate * m
        st = st * (ref_norm / jnp.sqrt(jnp.sum(st * st, axis=2, keepdims=True) + tiny_value))
        state[c] = st
        w[t + chunks] = st.astype(bf16)

        @pl.when(has_out)
        def _():
            weight_copy(t).start()

    def arrive(t):
        @pl.when(jnp.logical_not(mid))
        def _():
            weight_copy(t).wait_recv()

            @pl.when(has_out)
            def _():
                weight_copy(t).start()

    def outer(block, c, first):
        h, gg, gw = parts((block + 1) * chunks + c, qv[block], cv[block], rows_ref[block, 1:2])
        units = pl.ds(pl.multiple_of(c * unit, unit), unit)
        hid[units, :] = h
        for k, g in enumerate((gg[:unit], gg[unit:], gw)):
            tot[k, units, :] = g if first else tot[k, units, :] + g

    def write_out(block):
        tile = min(256, tokens)
        down = w[pl.ds((block + 1) * chunks, chunks), 2].reshape(chunks * unit, dim)
        for start in range(0, tokens, tile):
            fo[block, start:start + tile] = dot_tn(hid[:, start:start + tile], down).astype(bf16)
        pltpu.make_async_copy(fo.at[block], out_hbm.at[block], o_sem.at[block]).start()

    def step(t, carry):
        block = t // chunks
        c = lax.rem(t, chunks)

        @pl.when(t == chunks - 1)
        def _():
            for copy in later_in:
                copy.wait()

        @pl.when(t >= chunks)
        def _():
            arrive(t - chunks)
        h, gg, gw = parts(t, kv[block], vv[block], rows_ref[block, 0:1])
        acc[0:2] = gg.reshape(2, unit, dim)
        acc[2] = gw

        @pl.when(has_out)
        def _():
            recv_copy(0, t).wait_recv()
            acc[...] += rbuf[0, t].astype(f32)
        sbuf[t] = acc[...].astype(bf16)
        send_copy(t).start()

        @pl.when(jnp.logical_and(mid, t > 0))
        def _():
            finish(t - 1)

        @pl.when(t >= chunks)
        def _():
            outer(0, c, True)
        return carry

    lax.fori_loop(0, 2 * chunks, step, 0)

    @pl.when(mid)
    def _():
        finish(2 * chunks - 1)
    write_out(0)

    def last(c, carry):
        arrive(chunks + c)
        outer(1, c, False)
        return carry
    lax.fori_loop(0, chunks, last, 0)

    qo, lo = 0, 0
    q, wd = piece, dim
    places = []
    for k, (bit, how, q2, w2) in enumerate(stages):
        side, partner = partners[k]
        if how == "lane":
            keep_q, give_q = qo, qo
            keep_l, give_l = lo + side * w2, lo + (1 - side) * w2
        else:
            keep_q, give_q = qo + side * q2, qo + (1 - side) * q2
            keep_l, give_l = lo, lo

        def region(p, uo, ln, q2=q2, w2=w2):
            return (slice(None), pl.ds(pl.multiple_of(p * piece + uo, 16), q2), pl.ds(pl.multiple_of(ln, 128), w2))
        for p in range(n):
            sb[k][:, p] = tot[region(p, give_q, give_l)].astype(bf16)
        copy = pltpu.make_async_remote_copy(
            src_ref=sb[k], dst_ref=rb[k], send_sem=f_send.at[k], recv_sem=f_recv.at[k],
            device_id={"seq": partner}, device_id_type=MESH)
        lcopy = pltpu.make_async_remote_copy(
            src_ref=lev, dst_ref=levr.at[k], send_sem=l_send.at[k], recv_sem=l_recv.at[k],
            device_id={"seq": partner}, device_id_type=MESH)
        copy.start()
        lcopy.start()
        if k == 0:
            write_out(1)
        lcopy.wait()
        lev[...] = jnp.maximum(lev[...], levr[k])
        copy.wait()
        for p in range(n):
            where = region(p, keep_q, keep_l)
            tot[where] = tot[where] + rb[k][:, p].astype(f32)
        qo, lo, q, wd = keep_q, keep_l, q2, w2
        places.append((qo, lo, q, wd))

    for p in range(n):
        zs[p] = tot[:, pl.ds(pl.multiple_of(p * piece + qo, 16), q), pl.ds(pl.multiple_of(lo, 128), wd)].astype(bf16)
    spread = []
    for d in range(1, n):
        p = lax.rem(me + d, n)
        spread.append(pltpu.make_async_remote_copy(
            src_ref=zs.at[p], dst_ref=zr.at[d - 1], send_sem=z_send.at[d - 1], recv_sem=z_recv.at[d - 1],
            device_id={"tok": p}, device_id_type=MESH))
        spread.append(pltpu.make_async_remote_copy(
            src_ref=lev, dst_ref=levr.at[ns + d - 1], send_sem=y_send.at[d - 1], recv_sem=y_recv.at[d - 1],
            device_id={"tok": p}, device_id_type=MESH))
    for copy in spread:
        copy.start()
    total = tot[:, pl.ds(pl.multiple_of(me * piece + qo, 16), q), pl.ds(pl.multiple_of(lo, 128), wd)]
    for copy in spread:
        copy.wait()
    top = lev[...]
    for d in range(1, n):
        total = total + zr[d - 1].astype(f32)
        top = jnp.maximum(top, levr[ns + d - 1])
    level_ref[...] = top
    gat[:, pl.ds(pl.multiple_of(qo, 16), q), pl.ds(pl.multiple_of(lo, 128), wd)] = total.astype(bf16)
    for k in range(ns - 1, -1, -1):
        uo, ln, q2, w2 = places[k]
        mine = gat.at[:, pl.ds(pl.multiple_of(uo, 16), q2), pl.ds(pl.multiple_of(ln, 128), w2)]
        copy = pltpu.make_async_remote_copy(
            src_ref=mine, dst_ref=mine, send_sem=g_send.at[k], recv_sem=g_recv.at[k],
            device_id={"seq": partners[k][1]}, device_id_type=MESH)
        copy.start()
        copy.wait()
    grad_ref[...] = gat[...].astype(f32)

    def drain(t, carry):
        send_copy(t).wait_send()

        @pl.when(has_out)
        def _():
            weight_copy(t).wait_send()
        return carry
    lax.fori_loop(0, 2 * chunks, drain, 0)
    for block in range(2):
        pltpu.make_async_copy(fo.at[block], out_hbm.at[block], o_sem.at[block]).wait()


def per_device(
    keys, values, queries, token_rate, valid_count, loss_scale, w_gate, w_up, w_down, out_cotangent
):
    rows = keys.shape[2]
    blocks = keys.shape[1]
    dim = keys.shape[3]
    width = w_gate.shape[1]
    n = lax.axis_size("tok")
    nseq = lax.axis_size("seq")
    where = lax.axis_index("tok")
    piece = width // n
    unit = min(64, piece)
    chunks = width // unit
    stages, q, wd = plan_stages(nseq, piece, dim)
    ns = len(stages)
    positions = where * rows + jnp.arange(rows, dtype=jnp.int32)
    count = valid_count[0][:, None]
    mask = (positions[None] < count).astype(f32)
    factor = -(loss_scale[0] * token_rate[0] * mask / count.astype(f32))
    lanes = jnp.stack([factor, mask], axis=1)
    weights = jnp.stack([w_gate.T, w_up.T, w_down])
    weights = weights.reshape(3, chunks, unit, dim).transpose(1, 0, 2, 3)
    any_spec = pl.BlockSpec(memory_space=pl.ANY)
    vmem = pl.BlockSpec(memory_space=pltpu.VMEM)
    dma = pltpu.SemaphoreType.DMA
    scratch = [
        pltpu.VMEM((blocks, rows, dim), bf16), pltpu.VMEM((blocks, rows, dim), bf16),
        pltpu.VMEM((blocks, rows, dim), bf16), pltpu.VMEM((blocks, rows, dim), bf16),
        pltpu.VMEM((3 * chunks, 3, unit, dim), bf16),
        pltpu.VMEM((2 * chunks, 3, unit, dim), bf16),
        pltpu.VMEM((2, 2 * chunks, 3, unit, dim), bf16),
        pltpu.VMEM((chunks, 3, unit, dim), f32), pltpu.VMEM((chunks, 3, unit, dim), f32),
        pltpu.VMEM((3, unit, dim), f32),
        pltpu.VMEM((3, width, dim), f32),
        pltpu.VMEM((width, rows), bf16),
        pltpu.VMEM((blocks, rows, dim), bf16),
        pltpu.VMEM((2 * chunks, 1, unit), f32),
        pltpu.VMEM((ns + n - 1, 2 * chunks, 1, unit), f32),
        pltpu.VMEM((n, 3, q, wd), bf16), pltpu.VMEM((n - 1, 3, q, wd), bf16),
        pltpu.VMEM((3, piece, dim), bf16),
    ]
    scratch += [pltpu.VMEM((3, n, a, b), bf16) for _, _, a, b in stages] * 2
    scratch += [
        dma((7,)), dma((2 * chunks,)), dma((2, 2 * chunks)), dma((2 * chunks,)), dma((2 * chunks,)),
        dma((2,)), dma((ns,)), dma((ns,)), dma((ns,)), dma((ns,)), dma((ns,)), dma((ns,)),
        dma((n - 1,)), dma((n - 1,)), dma((n - 1,)), dma((n - 1,)),
    ]
    fast_out, grads, levels = pl.pallas_call(
        functools.partial(kernel, n, nseq, chunks, unit, stages),
        out_shape=(
            jax.ShapeDtypeStruct((blocks, rows, dim), bf16),
            jax.ShapeDtypeStruct((3, piece, dim), f32),
            jax.ShapeDtypeStruct((2 * chunks, 1, unit), f32),
        ),
        in_specs=[pl.BlockSpec(memory_space=pltpu.SMEM)] + [any_spec] * 5 + [vmem],
        out_specs=(any_spec, vmem, vmem),
        scratch_shapes=scratch,
        compiler_params=pltpu.CompilerParams(
            collective_id=0, has_side_effects=True, vmem_limit_bytes=60 * 2**20
        ),
    )(loss_scale, keys[0], values[0], queries[0], out_cotangent[0], weights, lanes)
    levels = lax.dynamic_slice_in_dim(levels.reshape(blocks, width), where * piece, piece, 1)
    return (fast_out[None], grads[0].T, grads[1].T, grads[2], levels)


def solution(mesh):
    placed = (
        P("seq", None, "tok", None),
        P("seq", None, "tok", None),
        P("seq", None, "tok", None),
        P("seq", None, "tok"),
        P("seq", None),
        P(),
        P(),
        P(),
        P(),
        P("seq", None, "tok", None),
    )
    return jax.shard_map(
        per_device,
        mesh=mesh,
        in_specs=placed,
        out_specs=(
            P("seq", None, "tok", None),
            P(None, "tok"),
            P(None, "tok"),
            P("tok", None),
            P(None, "tok"),
        ),
        check_vma=False,
    )
```

```python
import functools

import jax
import jax.numpy as jnp
from jax import lax
from jax.experimental import pallas as pl
from jax.experimental.pallas import tpu as pltpu
from jax.sharding import PartitionSpec as P

momentum_keep = 0.9
step_rate = 3.0
tiny_value = 1e-06
MESH = pl.DeviceIdType.MESH
f32 = jnp.float32
bf16 = jnp.bfloat16


def dot_nt(a, b):
    return lax.dot_general(a, b, (((1,), (1,)), ((), ())), preferred_element_type=f32)


def dot_nn(a, b):
    return lax.dot_general(a, b, (((1,), (0,)), ((), ())), preferred_element_type=f32)


def dot_tn(a, b):
    return lax.dot_general(a, b, (((0,), (0,)), ((), ())), preferred_element_type=f32)


def plan_stages(nseq, piece, width):
    stages = []
    q, w, bit = piece, width, 1
    while bit < nseq:
        if w > 128:
            w //= 2
            stages.append((bit, "lane", q, w))
        else:
            q //= 2
            stages.append((bit, "unit", q, w))
        bit *= 2
    return stages, q, w


def kernel(
    n, nseq, chunks, unit, stages,
    scale_ref, count_ref, keys, values, queries, cots, gate_in, up_in, down_in, rate_ref,
    out_hbm, gate_out, up_out, down_out, level_ref,
    kv, vv, qv, cv, wraw, rows_ref, w, sbuf, rbuf, state, mom, acc, tot, hid, fo, lev, levr, zs, zr, gat, *rest,
):
    ns = len(stages)
    sb, rb = rest[:ns], rest[ns:2 * ns]
    in_sem, s_send, s_recv, w_send, w_recv, o_sem, f_send, f_recv, l_send, l_recv, g_send, g_recv, z_send, z_recv, y_send, y_recv = rest[2 * ns:]
    dim = kv.shape[2]
    tokens = kv.shape[1]
    piece = chunks * unit // n
    me = lax.axis_index("tok")
    seq = lax.axis_index("seq")
    half = n // 2
    low = me < half
    inn = jnp.where(low, me + 1, me - 1)
    mid = jnp.logical_or(me == half - 1, me == half)
    has_out = jnp.logical_and(me > 0, me < n - 1)
    out = jnp.where(low, jnp.maximum(me - 1, 0), jnp.minimum(me + 1, n - 1))
    kind = jnp.where(mid, 1, 0)

    first_in = [
        pltpu.make_async_copy(keys.at[0], kv.at[0], in_sem.at[0]),
        pltpu.make_async_copy(gate_in, wraw.at[0], in_sem.at[1]),
        pltpu.make_async_copy(up_in, wraw.at[1], in_sem.at[7]),
        pltpu.make_async_copy(down_in, wraw.at[2], in_sem.at[8]),
        pltpu.make_async_copy(values.at[0], vv.at[0], in_sem.at[2]),
    ]
    later_in = [
        pltpu.make_async_copy(keys.at[1], kv.at[1], in_sem.at[3]),
        pltpu.make_async_copy(values.at[1], vv.at[1], in_sem.at[4]),
        pltpu.make_async_copy(queries, qv, in_sem.at[5]),
        pltpu.make_async_copy(cots, cv, in_sem.at[6]),
    ]
    for copy in first_in + later_in:
        copy.start()

    barrier = pltpu.get_barrier_semaphore()
    for d in range(1, n):
        pl.semaphore_signal(barrier, inc=1, device_id={"tok": lax.rem(me + d, n)}, device_id_type=MESH)
    partners = []
    for bit, _, _, _ in stages:
        side = lax.rem(seq // bit, 2)
        partner = seq + bit * (1 - 2 * side)
        partners.append((side, partner))
        pl.semaphore_signal(barrier, inc=1, device_id={"seq": partner}, device_id_type=MESH)
    pl.semaphore_wait(barrier, n - 1 + ns)

    lev[...] = jnp.zeros_like(lev)
    scale = scale_ref[0]
    slots = lax.broadcasted_iota(jnp.int32, (1, tokens), 1) + me * tokens
    for block in range(2):
        count = count_ref[0, block]
        mask = jnp.where(slots < count, 1.0, 0.0).astype(f32)
        rows_ref[block, 1:2] = mask
        rows_ref[block, 0:1] = -(scale * rate_ref[0, block:block + 1] * mask / count.astype(f32))
    for copy in first_in[1:4]:
        copy.wait()
    side_by = max(128, unit)
    for k in range(2):
        for start in range(0, chunks * unit, side_by):
            turned = wraw[k, :, start:start + side_by].T
            for off in range(0, side_by, unit):
                w[(start + off) // unit, k] = turned[off:off + unit]
    for c in range(chunks):
        w[c, 2] = wraw[2, c * unit:(c + 1) * unit]
    first_in[0].wait()
    first_in[4].wait()

    @pl.when(mid)
    def _():
        def fill(c, carry):
            state[c] = w[c].astype(f32)
            mom[c] = jnp.zeros(mom.shape[1:], f32)
            return carry
        lax.fori_loop(0, chunks, fill, 0)

    def send_copy(t):
        return pltpu.make_async_remote_copy(
            src_ref=sbuf.at[t], dst_ref=rbuf.at[kind, t], send_sem=s_send.at[t],
            recv_sem=s_recv.at[kind, t], device_id={"tok": inn}, device_id_type=MESH)

    def recv_copy(k, t):
        return pltpu.make_async_remote_copy(
            src_ref=sbuf.at[t], dst_ref=rbuf.at[k, t], send_sem=s_send.at[t],
            recv_sem=s_recv.at[k, t], device_id={"tok": inn}, device_id_type=MESH)

    def weight_copy(t):
        return pltpu.make_async_remote_copy(
            src_ref=w.at[t + chunks], dst_ref=w.at[t + chunks], send_sem=w_send.at[t],
            recv_sem=w_recv.at[t], device_id={"tok": out}, device_id_type=MESH)

    def parts(wt, x, e, row):
        ab = dot_nt(w[wt, 0:2].reshape(2 * unit, dim), x)
        r = dot_nt(w[wt, 2], e) * row
        a, b = ab[:unit], ab[unit:]
        s = jax.nn.sigmoid(a)
        g = a * s
        h = (g * b * row).astype(bf16)
        eb = (r * g).astype(bf16)
        ea = (r * b * s * (1.0 + a * (1.0 - s))).astype(bf16)
        gg = dot_nn(jnp.concatenate([ea, eb], axis=0), x)
        gw = dot_nn(h, e)
        return h, gg, gw

    def finish(t):
        c = lax.rem(t, chunks)
        recv_copy(1, t).wait_recv()
        s = sbuf[t].astype(f32) + rbuf[1, t].astype(f32)
        top = jnp.abs(s[0])
        top = functools.reduce(jnp.maximum, [top[:, k:k + 128] for k in range(0, dim, 128)])
        lev[t] = jnp.max(top.T, axis=0, keepdims=True)
        m = momentum_keep * mom[c] + s * (1.0 / scale)
        mom[c] = m
        first = w[c].astype(f32)
        ref_norm = jnp.sqrt(jnp.sum(first * first, axis=2, keepdims=True) + tiny_value)
        st = state[c] - step_rate * m
        st = st * (ref_norm / jnp.sqrt(jnp.sum(st * st, axis=2, keepdims=True) + tiny_value))
        state[c] = st
        w[t + chunks] = st.astype(bf16)

        @pl.when(has_out)
        def _():
            weight_copy(t).start()

    def arrive(t):
        @pl.when(jnp.logical_not(mid))
        def _():
            weight_copy(t).wait_recv()

            @pl.when(has_out)
            def _():
                weight_copy(t).start()

    def outer(block, c, first):
        h, gg, gw = parts((block + 1) * chunks + c, qv[block], cv[block], rows_ref[block, 1:2])
        units = pl.ds(pl.multiple_of(c * unit, unit), unit)
        hid[block, units, :] = h
        for k, g in enumerate((gg[:unit], gg[unit:], gw)):
            tot[k, units, :] = g if first else tot[k, units, :] + g

    def write_out(block):
        tile = min(256, tokens)
        down = w[pl.ds((block + 1) * chunks, chunks), 2].reshape(chunks * unit, dim)
        for start in range(0, tokens, tile):
            fo[block, start:start + tile] = dot_tn(hid[block, :, start:start + tile], down).astype(bf16)
        pltpu.make_async_copy(fo.at[block], out_hbm.at[0, block], o_sem.at[block]).start()

    places = []
    qo, lo = 0, 0
    for k, (bit, how, q2, w2) in enumerate(stages):
        side, _ = partners[k]
        if how == "lane":
            give = (qo, lo + (1 - side) * w2)
            lo = lo + side * w2
        else:
            give = (qo + (1 - side) * q2, lo)
            qo = qo + side * q2
        places.append((qo, lo, give, q2, w2))

    def region(p, uo, ln, k):
        return (slice(None), pl.ds(pl.multiple_of(p * piece + uo, 16), places[k][3]),
                pl.ds(pl.multiple_of(ln, 128), places[k][4]))

    def stage_copy(k, p):
        return pltpu.make_async_remote_copy(
            src_ref=sb[k].at[p], dst_ref=rb[k].at[p], send_sem=f_send.at[k, p],
            recv_sem=f_recv.at[k, p], device_id={"seq": partners[k][1]}, device_id_type=MESH)

    def stage_start(k, p):
        sb[k][p] = tot[region(p, places[k][2][0], places[k][2][1], k)].astype(bf16)
        stage_copy(k, p).start()

    def stage_end(k, p):
        stage_copy(k, p).wait()
        where = region(p, places[k][0], places[k][1], k)
        tot[where] = tot[where] + rb[k][p].astype(f32)

    def level_copy(k):
        return pltpu.make_async_remote_copy(
            src_ref=lev, dst_ref=levr.at[k], send_sem=l_send.at[k], recv_sem=l_recv.at[k],
            device_id={"seq": partners[k][1]}, device_id_type=MESH)

    lag = jnp.where(mid, 2, 4)
    each = piece // unit

    def step(t, carry):
        c = lax.rem(t, chunks)

        @pl.when(t == chunks - 1)
        def _():
            for copy in later_in:
                copy.wait()

        @pl.when(t < 2 * chunks)
        def _():
            block = t // chunks

            @pl.when(t >= chunks)
            def _():
                arrive(t - chunks)
            h, gg, gw = parts(t, kv[block], vv[block], rows_ref[block, 0:1])
            acc[0:2] = gg.reshape(2, unit, dim)
            acc[2] = gw

            @pl.when(has_out)
            def _():
                recv_copy(0, t).wait_recv()
                acc[...] += rbuf[0, t].astype(f32)
            sbuf[t] = acc[...].astype(bf16)
            send_copy(t).start()

        @pl.when(jnp.logical_and(mid, jnp.logical_and(t > 0, t <= 2 * chunks)))
        def _():
            finish(t - 1)

        @pl.when(jnp.logical_and(t >= chunks, t < 2 * chunks))
        def _():
            outer(0, c, True)

        @pl.when(t == 2 * chunks)
        def _():
            write_out(0)
        late = t - chunks - lag

        @pl.when(jnp.logical_and(late >= 0, late < chunks))
        def _():
            arrive(chunks + late)
            outer(1, late, False)
            p = late // each

            @pl.when(lax.rem(late, each) == each - 1)
            def _():
                stage_start(0, p)
                for k in range(1, ns + 1):
                    @pl.when(p >= k)
                    def _():
                        stage_end(k - 1, p - k)
                        if k < ns:
                            stage_start(k, p - k)
        return carry

    lax.fori_loop(0, 2 * chunks + 4, step, 0)

    for e in range(n, n + ns):
        level_copy(e - n).start()
        if e == n:
            write_out(1)
        for k in range(1, ns + 1):
            if 0 <= e - k < n:
                stage_end(k - 1, e - k)
                if k < ns:
                    stage_start(k, e - k)
        level_copy(e - n).wait()
        lev[...] = jnp.maximum(lev[...], levr[e - n])
    q, wd = places[-1][3], places[-1][4]

    for p in range(n):
        zs[p] = tot[:, pl.ds(pl.multiple_of(p * piece + qo, 16), q), pl.ds(pl.multiple_of(lo, 128), wd)].astype(bf16)
    spread = []
    for d in range(1, n):
        p = lax.rem(me + d, n)
        spread.append(pltpu.make_async_remote_copy(
            src_ref=zs.at[p], dst_ref=zr.at[d - 1], send_sem=z_send.at[d - 1], recv_sem=z_recv.at[d - 1],
            device_id={"tok": p}, device_id_type=MESH))
        spread.append(pltpu.make_async_remote_copy(
            src_ref=lev, dst_ref=levr.at[ns + d - 1], send_sem=y_send.at[d - 1], recv_sem=y_recv.at[d - 1],
            device_id={"tok": p}, device_id_type=MESH))
    for copy in spread:
        copy.start()
    total = tot[:, pl.ds(pl.multiple_of(me * piece + qo, 16), q), pl.ds(pl.multiple_of(lo, 128), wd)]
    for copy in spread:
        copy.wait()
    top = lev[...]
    for d in range(1, n):
        total = total + zr[d - 1].astype(f32)
        top = jnp.maximum(top, levr[ns + d - 1])
    lev[...] = top
    for block in range(2):
        for j in range(each):
            level_ref[block:block + 1, j * unit:(j + 1) * unit] = lev[block * chunks + me * each + j]
    gat[:, pl.ds(pl.multiple_of(qo, 16), q), pl.ds(pl.multiple_of(lo, 128), wd)] = total.astype(bf16)
    for k in range(ns - 1, -1, -1):
        uo, ln, _, q2, w2 = places[k]
        mine = gat.at[:, pl.ds(pl.multiple_of(uo, 16), q2), pl.ds(pl.multiple_of(ln, 128), w2)]
        copy = pltpu.make_async_remote_copy(
            src_ref=mine, dst_ref=mine, send_sem=g_send.at[k], recv_sem=g_recv.at[k],
            device_id={"seq": partners[k][1]}, device_id_type=MESH)
        copy.start()
        copy.wait()
    gate_out[...] = gat[0].astype(f32).T
    up_out[...] = gat[1].astype(f32).T
    down_out[...] = gat[2].astype(f32)

    def drain(t, carry):
        send_copy(t).wait_send()

        @pl.when(has_out)
        def _():
            weight_copy(t).wait_send()
        return carry
    lax.fori_loop(0, 2 * chunks, drain, 0)
    for block in range(2):
        pltpu.make_async_copy(fo.at[block], out_hbm.at[0, block], o_sem.at[block]).wait()


def per_device(
    keys, values, queries, token_rate, valid_count, loss_scale, w_gate, w_up, w_down, out_cotangent
):
    rows = keys.shape[2]
    blocks = keys.shape[1]
    dim = keys.shape[3]
    width = w_gate.shape[1]
    n = lax.axis_size("tok")
    nseq = lax.axis_size("seq")
    piece = width // n
    unit = min(64, piece)
    chunks = width // unit
    stages, q, wd = plan_stages(nseq, piece, dim)
    ns = len(stages)
    any_spec = pl.BlockSpec(memory_space=pl.ANY)
    vmem = pl.BlockSpec(memory_space=pltpu.VMEM)
    dma = pltpu.SemaphoreType.DMA
    scratch = [
        pltpu.VMEM((blocks, rows, dim), bf16), pltpu.VMEM((blocks, rows, dim), bf16),
        pltpu.VMEM((blocks, rows, dim), bf16), pltpu.VMEM((blocks, rows, dim), bf16),
        pltpu.VMEM((3, dim, width), bf16),
        pltpu.VMEM((blocks, 2, rows), f32),
        pltpu.VMEM((3 * chunks, 3, unit, dim), bf16),
        pltpu.VMEM((2 * chunks, 3, unit, dim), bf16),
        pltpu.VMEM((2, 2 * chunks, 3, unit, dim), bf16),
        pltpu.VMEM((chunks, 3, unit, dim), f32), pltpu.VMEM((chunks, 3, unit, dim), f32),
        pltpu.VMEM((3, unit, dim), f32),
        pltpu.VMEM((3, width, dim), f32),
        pltpu.VMEM((blocks, width, rows), bf16),
        pltpu.VMEM((blocks, rows, dim), bf16),
        pltpu.VMEM((2 * chunks, 1, unit), f32),
        pltpu.VMEM((ns + n - 1, 2 * chunks, 1, unit), f32),
        pltpu.VMEM((n, 3, q, wd), bf16), pltpu.VMEM((n - 1, 3, q, wd), bf16),
        pltpu.VMEM((3, piece, dim), bf16),
    ]
    scratch += [pltpu.VMEM((n, 3, a, b), bf16) for _, _, a, b in stages] * 2
    scratch += [
        dma((9,)), dma((2 * chunks,)), dma((2, 2 * chunks)), dma((2 * chunks,)), dma((2 * chunks,)),
        dma((2,)), dma((ns, n)), dma((ns, n)), dma((ns,)), dma((ns,)), dma((ns,)), dma((ns,)),
        dma((n - 1,)), dma((n - 1,)), dma((n - 1,)), dma((n - 1,)),
    ]
    smem = pl.BlockSpec(memory_space=pltpu.SMEM)
    return pl.pallas_call(
        functools.partial(kernel, n, nseq, chunks, unit, stages),
        out_shape=(
            jax.ShapeDtypeStruct((1, blocks, rows, dim), bf16),
            jax.ShapeDtypeStruct((dim, piece), f32),
            jax.ShapeDtypeStruct((dim, piece), f32),
            jax.ShapeDtypeStruct((piece, dim), f32),
            jax.ShapeDtypeStruct((blocks, piece), f32),
        ),
        in_specs=[smem] * 2 + [any_spec] * 7 + [vmem],
        out_specs=(any_spec, vmem, vmem, vmem, vmem),
        scratch_shapes=scratch,
        compiler_params=pltpu.CompilerParams(
            collective_id=0, has_side_effects=True, vmem_limit_bytes=60 * 2**20
        ),
    )(loss_scale, valid_count, keys[0], values[0], queries[0], out_cotangent[0],
      w_gate, w_up, w_down, token_rate)


def solution(mesh):
    placed = (
        P("seq", None, "tok", None),
        P("seq", None, "tok", None),
        P("seq", None, "tok", None),
        P("seq", None, "tok"),
        P("seq", None),
        P(),
        P(),
        P(),
        P(),
        P("seq", None, "tok", None),
    )
    return jax.shard_map(
        per_device,
        mesh=mesh,
        in_specs=placed,
        out_specs=(
            P("seq", None, "tok", None),
            P(None, "tok"),
            P(None, "tok"),
            P("tok", None),
            P(None, "tok"),
        ),
        check_vma=False,
    )
```

```python
import functools

import jax
import jax.numpy as jnp
from jax import lax
from jax.experimental import pallas as pl
from jax.experimental.pallas import tpu as pltpu
from jax.sharding import PartitionSpec as P

momentum_keep = 0.9
step_rate = 3.0
tiny_value = 1e-06
MESH = pl.DeviceIdType.MESH
f32 = jnp.float32
bf16 = jnp.bfloat16


def dot_nt(a, b):
    return lax.dot_general(a, b, (((1,), (1,)), ((), ())), preferred_element_type=f32)


def dot_nn(a, b):
    return lax.dot_general(a, b, (((1,), (0,)), ((), ())), preferred_element_type=f32)


def dot_tn(a, b):
    return lax.dot_general(a, b, (((0,), (0,)), ((), ())), preferred_element_type=f32)


def plan_stages(nseq, piece, width):
    stages = []
    q, w, bit = piece, width, 1
    while bit < nseq:
        if w > 128:
            w //= 2
            stages.append((bit, "lane", q, w))
        else:
            q //= 2
            stages.append((bit, "unit", q, w))
        bit *= 2
    return stages, q, w


def kernel(
    n, nseq, chunks, unit, stages,
    scale_ref, count_ref, keys, values, queries, cots, gate_in, up_in, down_in, rate_ref,
    out_hbm, gate_out, up_out, down_out, level_ref,
    kv, vv, qv, cv, wraw, rows_ref, w, sbuf, rbuf, state, mom, acc, tot, hid, fo, lev, levr, zs, zr, gat, *rest,
):
    ns = len(stages)
    sb, rb = rest[:ns], rest[ns:2 * ns]
    in_sem, s_send, s_recv, w_send, w_recv, o_sem, f_send, f_recv, l_send, l_recv, g_send, g_recv, z_send, z_recv, y_send, y_recv = rest[2 * ns:]
    dim = kv.shape[2]
    tokens = kv.shape[1]
    piece = chunks * unit // n
    me = lax.axis_index("tok")
    seq = lax.axis_index("seq")
    half = n // 2
    low = me < half
    inn = jnp.where(low, me + 1, me - 1)
    mid = jnp.logical_or(me == half - 1, me == half)
    has_out = jnp.logical_and(me > 0, me < n - 1)
    out = jnp.where(low, jnp.maximum(me - 1, 0), jnp.minimum(me + 1, n - 1))
    kind = jnp.where(mid, 1, 0)

    first_in = [
        pltpu.make_async_copy(keys.at[0], kv.at[0], in_sem.at[0]),
        pltpu.make_async_copy(gate_in, wraw.at[0], in_sem.at[1]),
        pltpu.make_async_copy(up_in, wraw.at[1], in_sem.at[7]),
        pltpu.make_async_copy(down_in, wraw.at[2], in_sem.at[8]),
        pltpu.make_async_copy(values.at[0], vv.at[0], in_sem.at[2]),
    ]
    later_in = [
        pltpu.make_async_copy(keys.at[1], kv.at[1], in_sem.at[3]),
        pltpu.make_async_copy(values.at[1], vv.at[1], in_sem.at[4]),
        pltpu.make_async_copy(queries, qv, in_sem.at[5]),
        pltpu.make_async_copy(cots, cv, in_sem.at[6]),
    ]
    for copy in first_in + later_in:
        copy.start()

    barrier = pltpu.get_barrier_semaphore()
    for d in range(1, n):
        pl.semaphore_signal(barrier, inc=1, device_id={"tok": lax.rem(me + d, n)}, device_id_type=MESH)
    partners = []
    for bit, _, _, _ in stages:
        side = lax.rem(seq // bit, 2)
        partner = seq + bit * (1 - 2 * side)
        partners.append((side, partner))
        pl.semaphore_signal(barrier, inc=1, device_id={"seq": partner}, device_id_type=MESH)
    pl.semaphore_wait(barrier, n - 1 + ns)

    lev[...] = jnp.zeros_like(lev)
    scale = scale_ref[0]
    slots = lax.broadcasted_iota(jnp.int32, (1, tokens), 1) + me * tokens
    for block in range(2):
        count = count_ref[0, block]
        mask = jnp.where(slots < count, 1.0, 0.0).astype(f32)
        rows_ref[block, 1:2] = mask
        rows_ref[block, 0:1] = -(scale * rate_ref[0, block:block + 1] * mask / count.astype(f32))
    for copy in first_in[1:4]:
        copy.wait()
    side_by = max(128, unit)
    for k in range(2):
        for start in range(0, chunks * unit, side_by):
            turned = wraw[k, :, start:start + side_by].T
            for off in range(0, side_by, unit):
                w[(start + off) // unit, k] = turned[off:off + unit]
    for c in range(chunks):
        w[c, 2] = wraw[2, c * unit:(c + 1) * unit]
    first_in[0].wait()
    first_in[4].wait()

    @pl.when(mid)
    def _():
        def fill(c, carry):
            state[c] = w[c].astype(f32)
            mom[c] = jnp.zeros(mom.shape[1:], f32)
            return carry
        lax.fori_loop(0, chunks, fill, 0)

    def send_copy(t):
        return pltpu.make_async_remote_copy(
            src_ref=sbuf.at[t], dst_ref=rbuf.at[kind, t], send_sem=s_send.at[t],
            recv_sem=s_recv.at[kind, t], device_id={"tok": inn}, device_id_type=MESH)

    def recv_copy(k, t):
        return pltpu.make_async_remote_copy(
            src_ref=sbuf.at[t], dst_ref=rbuf.at[k, t], send_sem=s_send.at[t],
            recv_sem=s_recv.at[k, t], device_id={"tok": inn}, device_id_type=MESH)

    def weight_copy(t):
        return pltpu.make_async_remote_copy(
            src_ref=w.at[t + chunks], dst_ref=w.at[t + chunks], send_sem=w_send.at[t],
            recv_sem=w_recv.at[t], device_id={"tok": out}, device_id_type=MESH)

    def parts(wt, x, e, row):
        ab = dot_nt(w[wt, 0:2].reshape(2 * unit, dim), x)
        r = dot_nt(w[wt, 2], e) * row
        a, b = ab[:unit], ab[unit:]
        s = jax.nn.sigmoid(a)
        g = a * s
        h = (g * b * row).astype(bf16)
        eb = (r * g).astype(bf16)
        ea = (r * b * s * (1.0 + a * (1.0 - s))).astype(bf16)
        gg = dot_nn(jnp.concatenate([ea, eb], axis=0), x)
        gw = dot_nn(h, e)
        return h, gg, gw

    def finish(t):
        c = lax.rem(t, chunks)
        recv_copy(1, t).wait_recv()
        s = sbuf[t].astype(f32) + rbuf[1, t].astype(f32)
        top = jnp.abs(s[0])
        top = functools.reduce(jnp.maximum, [top[:, k:k + 128] for k in range(0, dim, 128)])
        lev[t] = jnp.max(top.T, axis=0, keepdims=True)
        m = momentum_keep * mom[c] + s * (1.0 / scale)
        mom[c] = m
        first = w[c].astype(f32)
        ref_norm = jnp.sqrt(jnp.sum(first * first, axis=2, keepdims=True) + tiny_value)
        st = state[c] - step_rate * m
        st = st * (ref_norm / jnp.sqrt(jnp.sum(st * st, axis=2, keepdims=True) + tiny_value))
        state[c] = st
        w[t + chunks] = st.astype(bf16)

        @pl.when(has_out)
        def _():
            weight_copy(t).start()

    def arrive(t):
        @pl.when(jnp.logical_not(mid))
        def _():
            weight_copy(t).wait_recv()

            @pl.when(has_out)
            def _():
                weight_copy(t).start()

    def outer(block, c, first):
        h, gg, gw = parts((block + 1) * chunks + c, qv[block], cv[block], rows_ref[block, 1:2])
        units = pl.ds(pl.multiple_of(c * unit, unit), unit)
        hid[block, units, :] = h
        for k, g in enumerate((gg[:unit], gg[unit:], gw)):
            tot[k, units, :] = g if first else tot[k, units, :] + g

    def write_out(block):
        tile = min(256, tokens)
        down = w[pl.ds((block + 1) * chunks, chunks), 2].reshape(chunks * unit, dim)
        for start in range(0, tokens, tile):
            fo[block, start:start + tile] = dot_tn(hid[block, :, start:start + tile], down).astype(bf16)
        pltpu.make_async_copy(fo.at[block], out_hbm.at[0, block], o_sem.at[block]).start()

    places = []
    qo, lo = 0, 0
    for k, (bit, how, q2, w2) in enumerate(stages):
        side, _ = partners[k]
        if how == "lane":
            give = (qo, lo + (1 - side) * w2)
            lo = lo + side * w2
        else:
            give = (qo + (1 - side) * q2, lo)
            qo = qo + side * q2
        places.append((qo, lo, give, q2, w2))

    def region(p, uo, ln, k):
        return (slice(None), pl.ds(pl.multiple_of(p * piece + uo, 16), places[k][3]),
                pl.ds(pl.multiple_of(ln, 128), places[k][4]))

    def stage_copy(k, p):
        return pltpu.make_async_remote_copy(
            src_ref=sb[k].at[p], dst_ref=rb[k].at[p], send_sem=f_send.at[k, p],
            recv_sem=f_recv.at[k, p], device_id={"seq": partners[k][1]}, device_id_type=MESH)

    def stage_start(k, p):
        sb[k][p] = tot[region(p, places[k][2][0], places[k][2][1], k)].astype(bf16)
        stage_copy(k, p).start()

    def stage_end(k, p):
        stage_copy(k, p).wait()
        where = region(p, places[k][0], places[k][1], k)
        tot[where] = tot[where] + rb[k][p].astype(f32)

    def level_copy(k):
        return pltpu.make_async_remote_copy(
            src_ref=lev, dst_ref=levr.at[k], send_sem=l_send.at[k], recv_sem=l_recv.at[k],
            device_id={"seq": partners[k][1]}, device_id_type=MESH)

    lag = jnp.where(mid, 2, 4)
    each = piece // unit

    def step(t, carry):
        c = lax.rem(t, chunks)

        @pl.when(t == chunks - 1)
        def _():
            for copy in later_in:
                copy.wait()

        @pl.when(t < 2 * chunks)
        def _():
            block = t // chunks

            @pl.when(t >= chunks)
            def _():
                arrive(t - chunks)
            h, gg, gw = parts(t, kv[block], vv[block], rows_ref[block, 0:1])
            acc[0:2] = gg.reshape(2, unit, dim)
            acc[2] = gw

            @pl.when(has_out)
            def _():
                recv_copy(0, t).wait_recv()
                acc[...] += rbuf[0, t].astype(f32)
            sbuf[t] = acc[...].astype(bf16)
            send_copy(t).start()

        @pl.when(jnp.logical_and(t >= chunks, t < 2 * chunks))
        def _():
            outer(0, c, True)

        @pl.when(t == 2 * chunks)
        def _():
            write_out(0)

        @pl.when(jnp.logical_and(mid, jnp.logical_and(t > 0, t <= 2 * chunks)))
        def _():
            finish(t - 1)

        late = t - chunks - lag

        @pl.when(jnp.logical_and(late >= 0, late < chunks))
        def _():
            arrive(chunks + late)
            outer(1, late, False)
            p = late // each

            @pl.when(lax.rem(late, each) == each - 1)
            def _():
                stage_start(0, p)
                for k in range(1, ns + 1):
                    @pl.when(p >= k)
                    def _():
                        stage_end(k - 1, p - k)
                        if k < ns:
                            stage_start(k, p - k)
        return carry

    lax.fori_loop(0, 2 * chunks + 4, step, 0)

    for e in range(n, n + ns):
        level_copy(e - n).start()
        if e == n:
            write_out(1)
        for k in range(1, ns + 1):
            if 0 <= e - k < n:
                stage_end(k - 1, e - k)
                if k < ns:
                    stage_start(k, e - k)
        level_copy(e - n).wait()
        lev[...] = jnp.maximum(lev[...], levr[e - n])
    q, wd = places[-1][3], places[-1][4]

    for p in range(n):
        zs[p] = tot[:, pl.ds(pl.multiple_of(p * piece + qo, 16), q), pl.ds(pl.multiple_of(lo, 128), wd)].astype(bf16)
    spread = []
    for d in range(1, n):
        p = lax.rem(me + d, n)
        spread.append(pltpu.make_async_remote_copy(
            src_ref=zs.at[p], dst_ref=zr.at[d - 1], send_sem=z_send.at[d - 1], recv_sem=z_recv.at[d - 1],
            device_id={"tok": p}, device_id_type=MESH))
        spread.append(pltpu.make_async_remote_copy(
            src_ref=lev, dst_ref=levr.at[ns + d - 1], send_sem=y_send.at[d - 1], recv_sem=y_recv.at[d - 1],
            device_id={"tok": p}, device_id_type=MESH))
    for copy in spread:
        copy.start()
    total = tot[:, pl.ds(pl.multiple_of(me * piece + qo, 16), q), pl.ds(pl.multiple_of(lo, 128), wd)]
    for copy in spread:
        copy.wait()
    top = lev[...]
    for d in range(1, n):
        total = total + zr[d - 1].astype(f32)
        top = jnp.maximum(top, levr[ns + d - 1])
    lev[...] = top
    for block in range(2):
        for j in range(each):
            level_ref[block:block + 1, j * unit:(j + 1) * unit] = lev[block * chunks + me * each + j]
    gat[:, pl.ds(pl.multiple_of(qo, 16), q), pl.ds(pl.multiple_of(lo, 128), wd)] = total.astype(bf16)
    for k in range(ns - 1, -1, -1):
        uo, ln, _, q2, w2 = places[k]
        mine = gat.at[:, pl.ds(pl.multiple_of(uo, 16), q2), pl.ds(pl.multiple_of(ln, 128), w2)]
        copy = pltpu.make_async_remote_copy(
            src_ref=mine, dst_ref=mine, send_sem=g_send.at[k], recv_sem=g_recv.at[k],
            device_id={"seq": partners[k][1]}, device_id_type=MESH)
        copy.start()
        copy.wait()
    gate_out[...] = gat[0].astype(f32).T
    up_out[...] = gat[1].astype(f32).T
    down_out[...] = gat[2].astype(f32)

    def drain(t, carry):
        send_copy(t).wait_send()

        @pl.when(has_out)
        def _():
            weight_copy(t).wait_send()
        return carry
    lax.fori_loop(0, 2 * chunks, drain, 0)
    for block in range(2):
        pltpu.make_async_copy(fo.at[block], out_hbm.at[0, block], o_sem.at[block]).wait()


def per_device(
    keys, values, queries, token_rate, valid_count, loss_scale, w_gate, w_up, w_down, out_cotangent
):
    rows = keys.shape[2]
    blocks = keys.shape[1]
    dim = keys.shape[3]
    width = w_gate.shape[1]
    n = lax.axis_size("tok")
    nseq = lax.axis_size("seq")
    piece = width // n
    unit = min(64, piece)
    chunks = width // unit
    stages, q, wd = plan_stages(nseq, piece, dim)
    ns = len(stages)
    any_spec = pl.BlockSpec(memory_space=pl.ANY)
    vmem = pl.BlockSpec(memory_space=pltpu.VMEM)
    dma = pltpu.SemaphoreType.DMA
    scratch = [
        pltpu.VMEM((blocks, rows, dim), bf16), pltpu.VMEM((blocks, rows, dim), bf16),
        pltpu.VMEM((blocks, rows, dim), bf16), pltpu.VMEM((blocks, rows, dim), bf16),
        pltpu.VMEM((3, dim, width), bf16),
        pltpu.VMEM((blocks, 2, rows), f32),
        pltpu.VMEM((3 * chunks, 3, unit, dim), bf16),
        pltpu.VMEM((2 * chunks, 3, unit, dim), bf16),
        pltpu.VMEM((2, 2 * chunks, 3, unit, dim), bf16),
        pltpu.VMEM((chunks, 3, unit, dim), f32), pltpu.VMEM((chunks, 3, unit, dim), f32),
        pltpu.VMEM((3, unit, dim), f32),
        pltpu.VMEM((3, width, dim), f32),
        pltpu.VMEM((blocks, width, rows), bf16),
        pltpu.VMEM((blocks, rows, dim), bf16),
        pltpu.VMEM((2 * chunks, 1, unit), f32),
        pltpu.VMEM((ns + n - 1, 2 * chunks, 1, unit), f32),
        pltpu.VMEM((n, 3, q, wd), bf16), pltpu.VMEM((n - 1, 3, q, wd), bf16),
        pltpu.VMEM((3, piece, dim), bf16),
    ]
    scratch += [pltpu.VMEM((n, 3, a, b), bf16) for _, _, a, b in stages] * 2
    scratch += [
        dma((9,)), dma((2 * chunks,)), dma((2, 2 * chunks)), dma((2 * chunks,)), dma((2 * chunks,)),
        dma((2,)), dma((ns, n)), dma((ns, n)), dma((ns,)), dma((ns,)), dma((ns,)), dma((ns,)),
        dma((n - 1,)), dma((n - 1,)), dma((n - 1,)), dma((n - 1,)),
    ]
    smem = pl.BlockSpec(memory_space=pltpu.SMEM)
    return pl.pallas_call(
        functools.partial(kernel, n, nseq, chunks, unit, stages),
        out_shape=(
            jax.ShapeDtypeStruct((1, blocks, rows, dim), bf16),
            jax.ShapeDtypeStruct((dim, piece), f32),
            jax.ShapeDtypeStruct((dim, piece), f32),
            jax.ShapeDtypeStruct((piece, dim), f32),
            jax.ShapeDtypeStruct((blocks, piece), f32),
        ),
        in_specs=[smem] * 2 + [any_spec] * 7 + [vmem],
        out_specs=(any_spec, vmem, vmem, vmem, vmem),
        scratch_shapes=scratch,
        compiler_params=pltpu.CompilerParams(
            collective_id=0, has_side_effects=True, vmem_limit_bytes=60 * 2**20
        ),
    )(loss_scale, valid_count, keys[0], values[0], queries[0], out_cotangent[0],
      w_gate, w_up, w_down, token_rate)


def solution(mesh):
    placed = (
        P("seq", None, "tok", None),
        P("seq", None, "tok", None),
        P("seq", None, "tok", None),
        P("seq", None, "tok"),
        P("seq", None),
        P(),
        P(),
        P(),
        P(),
        P("seq", None, "tok", None),
    )
    return jax.shard_map(
        per_device,
        mesh=mesh,
        in_specs=placed,
        out_specs=(
            P("seq", None, "tok", None),
            P(None, "tok"),
            P(None, "tok"),
            P("tok", None),
            P(None, "tok"),
        ),
        check_vma=False,
    )
```
